32 devices in a mesh: seq: 8 (over z, x), head: 4 (over y, core).
Axes of the slice: x: 2, y: 2, z: 4, core: 2. Of those that a mesh axis runs over, the one named last changes fastest.
Arguments:
- inputs: bfloat16 [6144, 8192], P('seq', 'head'), may hold values from -6 to 6
- log_decay: float32 [128, 6144], P('head', 'seq'), may hold values from -3 to 0, as said below
- write_proj: bfloat16 [6144, 128], P('seq'), may hold values from -0.5 to 0.5
- read_proj: bfloat16 [6144, 128], P('seq'), may hold values from -0.5 to 0.5
- grad_out: bfloat16 [6144, 8192], P('seq', 'head'), may hold values from -0.75 to 0.75
Outputs:
- outputs: bfloat16 [6144, 8192], P('seq', 'head')
- grad_inputs: bfloat16 [6144, 8192], P('seq', 'head')
- grad_write: float32 [6144, 128], P(('seq', 'head'))
- grad_read: float32 [6144, 128], P(('seq', 'head'))
The draws below stay inside these ranges and needn't reach their ends.
Inputs may be any that keep to these rules, and one draw needn't show every extreme that they name: log_decay is negative everywhere.
All inputs are finite; a program needn't handle non-finite values.
Results may differ from the reference program's by a relative error of at most 0.0032.
Values sent between devices are 32-bit elements; how exact they have to be, the bound alone decides.
A program may use at most 192 MiB of HBM per device.

```python
import jax
import jax.numpy as jnp
from jax import lax

MIXER_HEADS = 128
HEAD_DIM = 64
STATE = 128
TOK_DEV = 768
SEQUENCE_TOKENS = 6144
INNER = 8192


def draw_log_decay(key, part):
    random_keys = jax.random.split(jax.random.fold_in(key, 17), 7)
    fast_share = 0.5
    is_fast = jax.random.uniform(random_keys[0], (MIXER_HEADS, 1)) < fast_share
    fast_rate = 1.0 / jax.random.uniform(random_keys[1], (MIXER_HEADS, 1), minval=30.0, maxval=50.0)
    slow_rate = jax.random.uniform(random_keys[2], (MIXER_HEADS, 1), minval=0.2, maxval=0.6) / SEQUENCE_TOKENS
    decay_speed = jnp.where(is_fast, fast_rate, slow_rate)
    sections = SEQUENCE_TOKENS // TOK_DEV
    section_divisor = jnp.exp(jax.random.uniform(random_keys[3], (MIXER_HEADS, sections, 1), minval=-0.7, maxval=0.7))
    section_divisor = jnp.broadcast_to(section_divisor, (MIXER_HEADS, sections, TOK_DEV)).reshape(MIXER_HEADS, SEQUENCE_TOKENS)
    token_divisor = jnp.exp(jax.random.uniform(random_keys[4], (MIXER_HEADS, SEQUENCE_TOKENS), minval=-0.7, maxval=0.7))
    section_offset = jax.random.randint(random_keys[5], (MIXER_HEADS, 4), 0, SEQUENCE_TOKENS)
    section_length = jax.random.uniform(random_keys[6], (MIXER_HEADS, 4), minval=0.22, maxval=0.69)
    token_position = jnp.arange(SEQUENCE_TOKENS, dtype=jnp.int32)
    section_count = jnp.zeros((MIXER_HEADS, SEQUENCE_TOKENS), jnp.float32)
    for token_index in range(4):
        section_count = section_count + jnp.where(token_position[None, :] == section_offset[:, token_index:token_index + 1], section_length[:, token_index:token_index + 1], 0.0)
    return -(decay_speed * section_divisor * token_divisor + section_count)


def block_levels(rng, extent, pieces, smallest, top_value):
    level, own = 1.0, jax.random.fold_in(rng, 6)
    for dim, shards_of in pieces:
        steps = jnp.exp(jax.random.uniform(jax.random.fold_in(own, dim), (shards_of,), jnp.float32, smallest / len(pieces), top_value / len(pieces)))
        level = level * jnp.repeat(steps, extent[dim] // shards_of).reshape([-1 if axis == dim else 1 for axis in range(len(extent))])
    return level


def centred(rng, shape, deviation, bound, cuts=(), kind=jnp.bfloat16):
    gain = block_levels(rng, shape, cuts, -0.22, 0.18) if cuts else 1.0
    drawn = jax.random.normal(rng, shape, jnp.float32) * deviation * gain
    return jnp.minimum(jnp.maximum(drawn, -bound), bound).astype(kind)


def setup_inputs(seed: int = 0) -> dict:
    splits = jax.random.split(jax.random.key(seed), 6)
    return {
        "inputs": centred(splits[0], (SEQUENCE_TOKENS, INNER), 1.0, 6.0, ((0, 8), (1, 4))),
        "log_decay": draw_log_decay(jax.random.fold_in(splits[5], 71), 0),
        "write_proj": centred(splits[2], (SEQUENCE_TOKENS, STATE), STATE ** -0.5, 0.5, ((0, 8),)),
        "read_proj": centred(splits[3], (SEQUENCE_TOKENS, STATE), STATE ** -0.5, 0.5, ((0, 8),)),
        "grad_out": centred(splits[4], (SEQUENCE_TOKENS, INNER), 0.125, 0.75, ((0, 8), (1, 4))),
    }


highest = lax.Precision.HIGHEST


def section_states(items):
    x_part, g_part, write_part, read_part, decay_part = items
    cumulative = jnp.cumsum(decay_part, axis=1)
    last_cumul = cumulative[:, -1:]
    tail_weight = jnp.exp(last_cumul - cumulative)
    lead_weight = jnp.exp(cumulative)
    x_wide = x_part.astype(jnp.float32)
    g_wide = g_part.astype(jnp.float32)
    local_state = jnp.einsum("jhp,jn->hpn", x_wide * tail_weight.T[:, :, None], write_part.astype(jnp.float32), precision=highest)
    local_grad = jnp.einsum("thp,tn->hpn", g_wide * lead_weight.T[:, :, None], read_part.astype(jnp.float32), precision=highest)
    return jnp.exp(last_cumul[:, 0]), local_state, local_grad


def section_outputs(items):
    x_part, g_part, write_part, read_part, decay_part, state_in, grad_state = items
    length = x_part.shape[0]
    cumulative = jnp.cumsum(decay_part, axis=1)
    last_cumul = cumulative[:, -1:]
    tail_weight = jnp.exp(last_cumul - cumulative)
    lead_weight = jnp.exp(cumulative)
    rows_index = lax.broadcasted_iota(jnp.int32, (length, length), 0)
    cols_index = lax.broadcasted_iota(jnp.int32, (length, length), 1)
    causal = rows_index >= cols_index
    differ = cumulative[:, :, None] - cumulative[:, None, :]
    decay_mat = jnp.exp(jnp.where(causal[None], differ, -jnp.inf))
    scores = jnp.dot(read_part, write_part.T, preferred_element_type=jnp.float32)
    mixing = (scores[None] * decay_mat).astype(jnp.bfloat16).astype(jnp.float32)
    x_wide = x_part.astype(jnp.float32)
    g_wide = g_part.astype(jnp.float32)
    write_wide = write_part.astype(jnp.float32)
    read_wide = read_part.astype(jnp.float32)
    y_intra = jnp.einsum("htj,jhp->thp", mixing, x_wide, precision=highest)
    y_inter = jnp.einsum("tn,hpn->thp", read_wide, state_in, precision=highest) * lead_weight.T[:, :, None]
    outputs = (y_intra + y_inter).astype(jnp.bfloat16).reshape(length, -1)
    grad_prod = jnp.einsum("thp,jhp->htj", g_wide, x_wide, precision=highest)
    grad_score = jnp.sum(grad_prod * decay_mat, axis=0)
    dx_intra = jnp.einsum("htj,thp->jhp", mixing, g_wide, precision=highest)
    dx_inter = jnp.einsum("jn,hpn->jhp", write_wide, grad_state, precision=highest) * tail_weight.T[:, :, None]
    grad_inputs = (dx_intra + dx_inter).astype(jnp.bfloat16).reshape(length, -1)
    grad_write = jnp.dot(grad_score.T, read_wide, precision=highest) + jnp.einsum("jhp,hpn->jn", x_wide * tail_weight.T[:, :, None], grad_state, precision=highest)
    grad_read = jnp.dot(grad_score, write_wide, precision=highest) + jnp.einsum("thp,hpn->tn", g_wide * lead_weight.T[:, :, None], state_in, precision=highest)
    return outputs, grad_inputs, grad_write, grad_read


def carry_step(carry, item):
    total, local = item
    return total[:, None, None] * carry + local, carry


def reference(inputs, log_decay, write_proj, read_proj, grad_out):
    sections = SEQUENCE_TOKENS // TOK_DEV
    x_sec = inputs.reshape(sections, TOK_DEV, MIXER_HEADS, HEAD_DIM)
    g_sec = grad_out.reshape(sections, TOK_DEV, MIXER_HEADS, HEAD_DIM)
    write_sec = write_proj.reshape(sections, TOK_DEV, STATE)
    read_sec = read_proj.reshape(sections, TOK_DEV, STATE)
    decay_sec = log_decay.reshape(MIXER_HEADS, sections, TOK_DEV).transpose(1, 0, 2)
    totals, local_states, local_grads = lax.map(section_states, (x_sec, g_sec, write_sec, read_sec, decay_sec))
    zero_block = jnp.zeros((MIXER_HEADS, HEAD_DIM, STATE), jnp.float32)
    _, state_in = lax.scan(carry_step, zero_block, (totals, local_states))
    _, grad_state = lax.scan(carry_step, zero_block, (totals, local_grads), reverse=True)
    outputs, grad_inputs, grad_write, grad_read = lax.map(section_outputs, (x_sec, g_sec, write_sec, read_sec, decay_sec, state_in, grad_state))
    return (outputs.reshape(SEQUENCE_TOKENS, MIXER_HEADS * HEAD_DIM), grad_inputs.reshape(SEQUENCE_TOKENS, MIXER_HEADS * HEAD_DIM), grad_write.reshape(SEQUENCE_TOKENS, STATE), grad_read.reshape(SEQUENCE_TOKENS, STATE))
```

```python
import functools

import jax
import jax.numpy as jnp
from jax import lax
from jax.experimental import pallas as pl
from jax.experimental.pallas import tpu as pltpu
from jax.sharding import PartitionSpec as P

CHUNK = 128
LANES = 128
PARTS = 2
LAG = 2
MESH = pl.DeviceIdType.MESH
F32 = jnp.float32
BF16 = jnp.bfloat16


def dot(a, b, dims):
    return lax.dot_general(a, b, ((dims[0], dims[1]), ((), ())), preferred_element_type=F32)


def split(value):
    high = value.astype(BF16)
    return high, (value - high.astype(F32)).astype(BF16)


def kernel(
    sections, head_size,
    x_ref, g_ref, w_ref, r_ref, cum_ref,
    y_ref, dx_ref, grads_ref,
    decay_ref, y_acc, dx_acc, scores_ref, gscore_ref,
    local_s, local_g, in_s, in_g, out_s, out_g,
    send_s, recv_s, send_g, recv_g,
):
    tokens, width = x_ref.shape
    state = w_ref.shape[1]
    packs = width // LANES
    each = LANES // head_size
    chunks = tokens // CHUNK
    units = packs * PARTS
    part_rows = state // PARTS
    me = lax.axis_index("seq")
    back = sections - 1 - me
    has_prev = me > 0
    has_next = me < sections - 1

    barrier = pltpu.get_barrier_semaphore()

    @pl.when(has_prev)
    def _():
        pl.semaphore_signal(barrier, inc=1, device_id={"seq": me - 1}, device_id_type=MESH)

    @pl.when(has_next)
    def _():
        pl.semaphore_signal(barrier, inc=1, device_id={"seq": me + 1}, device_id_type=MESH)

    pl.semaphore_wait(barrier, has_prev.astype(jnp.int32) + has_next.astype(jnp.int32))

    def state_copy(unit):
        pack, rows = unit // PARTS, pl.ds((unit % PARTS) * part_rows, part_rows)
        return pltpu.make_async_remote_copy(
            src_ref=out_s.at[pack, rows],
            dst_ref=in_s.at[pack, rows],
            send_sem=send_s.at[unit],
            recv_sem=recv_s.at[unit],
            device_id={"seq": me + 1},
            device_id_type=MESH,
        )

    def grad_copy(unit):
        pack, rows = unit // PARTS, pl.ds((unit % PARTS) * part_rows, part_rows)
        return pltpu.make_async_remote_copy(
            src_ref=out_g.at[pack, rows],
            dst_ref=in_g.at[pack, rows],
            send_sem=send_g.at[unit],
            recv_sem=recv_g.at[unit],
            device_id={"seq": me - 1},
            device_id_type=MESH,
        )

    @pl.when(me == 0)
    def _():
        in_s[...] = jnp.zeros_like(in_s)

    @pl.when(back == 0)
    def _():
        in_g[...] = jnp.zeros_like(in_g)

    grads_ref[...] = jnp.zeros_like(grads_ref)
    gscore_ref[...] = jnp.zeros_like(gscore_ref)
    for k in range(chunks):
        rows = slice(k * CHUNK, (k + 1) * CHUNK)
        scores_ref[k] = dot(r_ref[rows, :], w_ref[rows, :], ((1,), (1,)))

    lane_head = lax.broadcasted_iota(jnp.int32, (CHUNK, LANES), 1) // head_size
    causal = lax.broadcasted_iota(jnp.int32, (CHUNK, CHUNK), 0) >= lax.broadcasted_iota(
        jnp.int32, (CHUNK, CHUNK), 1
    )

    def only(value, head):
        return jnp.where(lane_head == head, value, jnp.zeros_like(value))

    def local(pack):
        lanes = pl.ds(pl.multiple_of(pack * LANES, LANES), LANES)
        before = jnp.zeros((1, LANES), F32)
        carried = jnp.zeros((state, LANES), F32)
        tails, scaled_x, scaled_g, lasts = [], [], [], []
        for k in range(chunks):
            rows = slice(k * CHUNK, (k + 1) * CHUNK)
            cum_rows = cum_ref[pack, :, rows]
            spread = jnp.concatenate(
                [jnp.broadcast_to(cum_rows[h : h + 1], (head_size, CHUNK)) for h in range(each)], axis=0
            )
            decay = spread.T
            decay_ref[rows, lanes] = decay
            last = decay[CHUNK - 1 : CHUNK]
            lead = jnp.exp(decay - before)
            tail = jnp.exp(last - decay)
            x = x_ref[rows, lanes]
            g = g_ref[rows, lanes]
            x_tail = (x.astype(F32) * tail).astype(BF16)
            g_lead = (g.astype(F32) * lead).astype(BF16)
            x_heads = jnp.concatenate([only(x, h) for h in range(each)], axis=0)
            g_heads = jnp.concatenate([only(g, h) for h in range(each)], axis=0)
            product = dot(g, x_heads, ((1,), (1,)))
            mixes, gained = [], gscore_ref[k]
            for h in range(each):
                column = decay[:, h * head_size : h * head_size + 1]
                matrix = jnp.exp(jnp.where(causal, column - cum_rows[h : h + 1], -jnp.inf))
                mixes.append((scores_ref[k] * matrix).astype(BF16))
                gained = gained + product[:, h * CHUNK : (h + 1) * CHUNK] * matrix
            gscore_ref[k] = gained
            y = dot(jnp.concatenate(mixes, axis=1), x_heads, ((1,), (0,)))
            dx = dot(jnp.concatenate(mixes, axis=0), g_heads, ((0,), (0,)))
            dx_acc[rows, lanes] = dx
            if k:
                high, low = split(carried)
                r = r_ref[rows, :]
                y = y + lead * dot(
                    jnp.concatenate([r, r], axis=1), jnp.concatenate([high, low], axis=0), ((1,), (0,))
                )
                grads_ref[rows, state:] += dot(g_lead, high, ((1,), (1,)))
            y_acc[rows, lanes] = y
            carried = jnp.exp(last - before) * carried + dot(w_ref[rows, :], x_tail, ((0,), (0,)))
            lasts.append(jnp.exp(last - before))
            tails.append(tail)
            scaled_x.append(x_tail)
            scaled_g.append(g_lead)
            before = last
        local_s[pack] = carried
        carried = jnp.zeros((state, LANES), F32)
        for k in reversed(range(chunks)):
            rows = slice(k * CHUNK, (k + 1) * CHUNK)
            if k < chunks - 1:
                high, low = split(carried)
                w = w_ref[rows, :]
                dx_acc[rows, lanes] += tails[k] * dot(
                    jnp.concatenate([w, w], axis=1), jnp.concatenate([high, low], axis=0), ((1,), (0,))
                )
                grads_ref[rows, :state] += dot(scaled_x[k], high, ((1,), (1,)))
            carried = lasts[k] * carried + dot(r_ref[rows, :], scaled_g[k], ((0,), (0,)))
        local_g[pack] = carried

    def finish_state(pack):
        lanes = pl.ds(pl.multiple_of(pack * LANES, LANES), LANES)
        high, low = split(in_s[pack])
        both = jnp.concatenate([high, low], axis=0)
        for k in range(chunks):
            rows = slice(k * CHUNK, (k + 1) * CHUNK)
            r = r_ref[rows, :]
            lead = jnp.exp(decay_ref[rows, lanes])
            carried = dot(jnp.concatenate([r, r], axis=1), both, ((1,), (0,)))
            y_ref[rows, lanes] = (y_acc[rows, lanes] + lead * carried).astype(y_ref.dtype)
            g_lead = (g_ref[rows, lanes].astype(F32) * lead).astype(BF16)
            grads_ref[rows, state:] += dot(g_lead, high, ((1,), (1,)))

    def finish_grad(pack):
        lanes = pl.ds(pl.multiple_of(pack * LANES, LANES), LANES)
        high, low = split(in_g[pack])
        both = jnp.concatenate([high, low], axis=0)
        last = decay_ref[tokens - 1 : tokens, lanes]
        for k in range(chunks):
            rows = slice(k * CHUNK, (k + 1) * CHUNK)
            w = w_ref[rows, :]
            tail = jnp.exp(last - decay_ref[rows, lanes])
            carried = dot(jnp.concatenate([w, w], axis=1), both, ((1,), (0,)))
            dx_ref[rows, lanes] = (dx_acc[rows, lanes] + tail * carried).astype(dx_ref.dtype)
            x_tail = (x_ref[rows, lanes].astype(F32) * tail).astype(BF16)
            grads_ref[rows, :state] += dot(x_tail, high, ((1,), (1,)))

    def step(turn, nothing):
        @pl.when(jnp.logical_and(turn % PARTS == 0, turn < units))
        def _():
            local(turn // PARTS)

        unit_s = turn - LAG * me
        unit_g = turn - LAG * back

        def live(unit):
            return jnp.logical_and(unit >= 0, unit < units)

        def pass_on(unit, has_source, has_target, copy, held, local_ref, out_ref):
            pack, rows = unit // PARTS, pl.ds((unit % PARTS) * part_rows, part_rows)
            lanes = pl.ds(pl.multiple_of(pack * LANES, LANES), LANES)

            @pl.when(has_source)
            def _():
                copy(unit).wait_recv()

            @pl.when(has_target)
            def _():
                total = jnp.exp(decay_ref[tokens - 1 : tokens, lanes])
                out_ref[pack, rows] = total * held[pack, rows] + local_ref[pack, rows]
                copy(unit).start()

        @pl.when(live(unit_s))
        def _():
            pass_on(unit_s, has_prev, has_next, state_copy, in_s, local_s, out_s)

        @pl.when(live(unit_g))
        def _():
            pass_on(unit_g, has_next, has_prev, grad_copy, in_g, local_g, out_g)

        @pl.when(jnp.logical_and(live(unit_s), unit_s % PARTS == PARTS - 1))
        def _():
            finish_state(unit_s // PARTS)

        @pl.when(jnp.logical_and(live(unit_g), unit_g % PARTS == PARTS - 1))
        def _():
            finish_grad(unit_g // PARTS)

        return nothing

    lax.fori_loop(0, units + LAG * (sections - 1), step, 0)

    for k in range(chunks):
        rows = slice(k * CHUNK, (k + 1) * CHUNK)
        high, low = split(gscore_ref[k])
        r = r_ref[rows, :]
        w = w_ref[rows, :]
        grads_ref[rows, :state] += dot(
            jnp.concatenate([high, low], axis=0), jnp.concatenate([r, r], axis=0), ((0,), (0,))
        )
        grads_ref[rows, state:] += dot(
            jnp.concatenate([high, low], axis=1), jnp.concatenate([w, w], axis=0), ((1,), (0,))
        )

    def drain(unit, nothing):
        @pl.when(has_next)
        def _():
            state_copy(unit).wait_send()

        @pl.when(has_prev)
        def _():
            grad_copy(unit).wait_send()

        return nothing

    lax.fori_loop(0, units, drain, 0)


def per_device(inputs, log_decay, write_proj, read_proj, grad_out):
    tokens, width = inputs.shape
    heads = log_decay.shape[0]
    state = write_proj.shape[1]
    sections = lax.axis_size("seq")
    head_size = width // heads
    packs = width // LANES
    chunks = tokens // CHUNK
    units = packs * PARTS
    cumulative = jnp.cumsum(log_decay, axis=1).reshape(packs, LANES // head_size, tokens)
    vmem = pl.BlockSpec(memory_space=pltpu.VMEM)
    block = pltpu.VMEM((packs, state, LANES), F32)
    outputs, grad_inputs, grads = pl.pallas_call(
        functools.partial(kernel, sections, head_size),
        out_shape=(
            jax.ShapeDtypeStruct((tokens, width), BF16),
            jax.ShapeDtypeStruct((tokens, width), BF16),
            jax.ShapeDtypeStruct((tokens, 2 * state), F32),
        ),
        in_specs=[vmem] * 5,
        out_specs=(vmem, vmem, vmem),
        scratch_shapes=[
            pltpu.VMEM((tokens, width), F32),
            pltpu.VMEM((tokens, width), F32),
            pltpu.VMEM((tokens, width), F32),
            pltpu.VMEM((chunks, CHUNK, CHUNK), F32),
            pltpu.VMEM((chunks, CHUNK, CHUNK), F32),
            block, block, block, block, block, block,
            pltpu.SemaphoreType.DMA((units,)),
            pltpu.SemaphoreType.DMA((units,)),
            pltpu.SemaphoreType.DMA((units,)),
            pltpu.SemaphoreType.DMA((units,)),
        ],
        compiler_params=pltpu.CompilerParams(
            collective_id=0, has_side_effects=True, vmem_limit_bytes=56 * 1024 * 1024
        ),
    )(inputs, grad_out, write_proj, read_proj, cumulative)
    summed = lax.psum_scatter(grads, "head", scatter_dimension=0, tiled=True)
    return outputs, grad_inputs, summed[:, :state], summed[:, state:]


def solution(mesh):
    return jax.shard_map(
        per_device,
        mesh=mesh,
        in_specs=(
            P("seq", "head"),
            P("head", "seq"),
            P("seq", None),
            P("seq", None),
            P("seq", "head"),
        ),
        out_specs=(
            P("seq", "head"),
            P("seq", "head"),
            P(("seq", "head"), None),
            P(("seq", "head"), None),
        ),
        check_vma=False,
    )
```

```python
import functools

import jax
import jax.numpy as jnp
from jax import lax
from jax.experimental import pallas as pl
from jax.experimental.pallas import tpu as pltpu
from jax.sharding import PartitionSpec as P

CHUNK = 128
LANES = 128
PARTS = 2
LAG = 3
MESH = pl.DeviceIdType.MESH
F32 = jnp.float32
BF16 = jnp.bfloat16


def dot(a, b, dims):
    return lax.dot_general(a, b, ((dims[0], dims[1]), ((), ())), preferred_element_type=F32)


def split(value):
    high = value.astype(BF16)
    return high, (value - high.astype(F32)).astype(BF16)


def twice(shared, high, low):
    return dot(
        jnp.concatenate([shared, shared], axis=0), jnp.concatenate([high, low], axis=0), ((0,), (0,))
    )


def kernel(
    sections, group, head_size,
    x_ref, g_ref, w_ref, r_ref, cum_ref,
    y_ref, dx_ref, gw_ref, gr_ref,
    grads_ref, landed_ref, decay_ref, y_acc, dx_acc, scores_ref, gscore_ref,
    local_s, local_g, in_s, in_g, out_s, out_g,
    send_s, recv_s, send_g, recv_g, send_h, recv_h,
):
    tokens, width = x_ref.shape
    state = w_ref.shape[1]
    packs = width // LANES
    each = LANES // head_size
    chunks = tokens // CHUNK
    units = packs * PARTS
    part_rows = state // PARTS
    me = lax.axis_index("seq")
    back = sections - 1 - me
    has_prev = me > 0
    has_next = me < sections - 1

    barrier = pltpu.get_barrier_semaphore()

    @pl.when(has_prev)
    def _():
        pl.semaphore_signal(barrier, inc=1, device_id={"seq": me - 1}, device_id_type=MESH)

    @pl.when(has_next)
    def _():
        pl.semaphore_signal(barrier, inc=1, device_id={"seq": me + 1}, device_id_type=MESH)

    mine = lax.axis_index("head")
    for gap in range(1, group):
        pl.semaphore_signal(
            barrier, inc=1, device_id={"head": lax.rem(mine + gap, group)}, device_id_type=MESH
        )
    pl.semaphore_wait(
        barrier, has_prev.astype(jnp.int32) + has_next.astype(jnp.int32) + (group - 1)
    )

    def state_copy(unit):
        pack, rows = unit // PARTS, pl.ds((unit % PARTS) * part_rows, part_rows)
        return pltpu.make_async_remote_copy(
            src_ref=out_s.at[pack, rows],
            dst_ref=in_s.at[pack, rows],
            send_sem=send_s.at[unit],
            recv_sem=recv_s.at[unit],
            device_id={"seq": me + 1},
            device_id_type=MESH,
        )

    def grad_copy(unit):
        pack, rows = unit // PARTS, pl.ds((unit % PARTS) * part_rows, part_rows)
        return pltpu.make_async_remote_copy(
            src_ref=out_g.at[pack, rows],
            dst_ref=in_g.at[pack, rows],
            send_sem=send_g.at[unit],
            recv_sem=recv_g.at[unit],
            device_id={"seq": me - 1},
            device_id_type=MESH,
        )

    @pl.when(me == 0)
    def _():
        in_s[...] = jnp.zeros_like(in_s)

    @pl.when(back == 0)
    def _():
        in_g[...] = jnp.zeros_like(in_g)

    grads_ref[...] = jnp.zeros_like(grads_ref)
    gscore_ref[...] = jnp.zeros_like(gscore_ref)
    for k in range(chunks):
        rows = slice(k * CHUNK, (k + 1) * CHUNK)
        scores_ref[k] = dot(r_ref[rows, :], w_ref[rows, :], ((1,), (1,)))

    lane_head = lax.broadcasted_iota(jnp.int32, (CHUNK, LANES), 1) // head_size
    causal = lax.broadcasted_iota(jnp.int32, (CHUNK, CHUNK), 0) >= lax.broadcasted_iota(
        jnp.int32, (CHUNK, CHUNK), 1
    )

    def only(value, head):
        return jnp.where(lane_head == head, value, jnp.zeros_like(value))

    def local(pack):
        lanes = pl.ds(pl.multiple_of(pack * LANES, LANES), LANES)
        before = jnp.zeros((1, LANES), F32)
        carried = jnp.zeros((state, LANES), F32)
        tails, scaled_x, scaled_g, rest_g, lasts = [], [], [], [], []
        for k in range(chunks):
            rows = slice(k * CHUNK, (k + 1) * CHUNK)
            cum_rows = cum_ref[pack, :, rows]
            spread = jnp.concatenate(
                [jnp.broadcast_to(cum_rows[h : h + 1], (head_size, CHUNK)) for h in range(each)], axis=0
            )
            decay = spread.T
            decay_ref[rows, lanes] = decay
            last = decay[CHUNK - 1 : CHUNK]
            lead = jnp.exp(decay - before)
            tail = jnp.exp(last - decay)
            x = x_ref[rows, lanes]
            g = g_ref[rows, lanes]
            x_tail, x_rest = split(x.astype(F32) * tail)
            g_lead, g_rest = split(g.astype(F32) * lead)
            x_heads = jnp.concatenate([only(x, h) for h in range(each)], axis=0)
            g_heads = jnp.concatenate([only(g, h) for h in range(each)], axis=0)
            product = dot(g, x_heads, ((1,), (1,)))
            mixes, gained = [], gscore_ref[k]
            for h in range(each):
                column = decay[:, h * head_size : h * head_size + 1]
                matrix = jnp.exp(jnp.where(causal, column - cum_rows[h : h + 1], -jnp.inf))
                mixes.append((scores_ref[k] * matrix).astype(BF16))
                gained = gained + product[:, h * CHUNK : (h + 1) * CHUNK] * matrix
            gscore_ref[k] = gained
            y = dot(jnp.concatenate(mixes, axis=1), x_heads, ((1,), (0,)))
            dx = dot(jnp.concatenate(mixes, axis=0), g_heads, ((0,), (0,)))
            dx_acc[rows, lanes] = dx
            if k:
                high, low = split(carried)
                r = r_ref[rows, :]
                y = y + lead * dot(
                    jnp.concatenate([r, r], axis=1), jnp.concatenate([high, low], axis=0), ((1,), (0,))
                )
                grads_ref[rows, state:] += dot(g_lead, high, ((1,), (1,)))
            y_acc[rows, lanes] = y
            carried = jnp.exp(last - before) * carried + twice(w_ref[rows, :], x_tail, x_rest)
            lasts.append(jnp.exp(last - before))
            tails.append(tail)
            scaled_x.append(x_tail)
            scaled_g.append(g_lead)
            rest_g.append(g_rest)
            before = last
        local_s[pack] = carried
        carried = jnp.zeros((state, LANES), F32)
        for k in reversed(range(chunks)):
            rows = slice(k * CHUNK, (k + 1) * CHUNK)
            if k < chunks - 1:
                high, low = split(carried)
                w = w_ref[rows, :]
                dx_acc[rows, lanes] += tails[k] * dot(
                    jnp.concatenate([w, w], axis=1), jnp.concatenate([high, low], axis=0), ((1,), (0,))
                )
                grads_ref[rows, :state] += dot(scaled_x[k], high, ((1,), (1,)))
            carried = lasts[k] * carried + twice(r_ref[rows, :], scaled_g[k], rest_g[k])
        local_g[pack] = carried

    def finish_state(pack):
        lanes = pl.ds(pl.multiple_of(pack * LANES, LANES), LANES)
        high, low = split(in_s[pack])
        both = jnp.concatenate([high, low], axis=0)
        for k in range(chunks):
            rows = slice(k * CHUNK, (k + 1) * CHUNK)
            r = r_ref[rows, :]
            lead = jnp.exp(decay_ref[rows, lanes])
            carried = dot(jnp.concatenate([r, r], axis=1), both, ((1,), (0,)))
            y_ref[rows, lanes] = (y_acc[rows, lanes] + lead * carried).astype(y_ref.dtype)
            g_lead = (g_ref[rows, lanes].astype(F32) * lead).astype(BF16)
            grads_ref[rows, state:] += dot(g_lead, high, ((1,), (1,)))

    def finish_grad(pack):
        lanes = pl.ds(pl.multiple_of(pack * LANES, LANES), LANES)
        high, low = split(in_g[pack])
        both = jnp.concatenate([high, low], axis=0)
        last = decay_ref[tokens - 1 : tokens, lanes]
        for k in range(chunks):
            rows = slice(k * CHUNK, (k + 1) * CHUNK)
            w = w_ref[rows, :]
            tail = jnp.exp(last - decay_ref[rows, lanes])
            carried = dot(jnp.concatenate([w, w], axis=1), both, ((1,), (0,)))
            dx_ref[rows, lanes] = (dx_acc[rows, lanes] + tail * carried).astype(dx_ref.dtype)
            x_tail = (x_ref[rows, lanes].astype(F32) * tail).astype(BF16)
            grads_ref[rows, :state] += dot(x_tail, high, ((1,), (1,)))

    def step(turn, nothing):
        @pl.when(jnp.logical_and(turn % PARTS == 0, turn < units))
        def _():
            local(turn // PARTS)

        unit_s = turn - LAG * me
        unit_g = turn - LAG * back

        def live(unit):
            return jnp.logical_and(unit >= 0, unit < units)

        def pass_on(unit, has_source, has_target, copy, held, local_ref, out_ref):
            pack, rows = unit // PARTS, pl.ds((unit % PARTS) * part_rows, part_rows)
            lanes = pl.ds(pl.multiple_of(pack * LANES, LANES), LANES)

            @pl.when(has_source)
            def _():
                copy(unit).wait_recv()

            @pl.when(has_target)
            def _():
                total = jnp.exp(decay_ref[tokens - 1 : tokens, lanes])
                out_ref[pack, rows] = total * held[pack, rows] + local_ref[pack, rows]
                copy(unit).start()

        @pl.when(live(unit_s))
        def _():
            pass_on(unit_s, has_prev, has_next, state_copy, in_s, local_s, out_s)

        @pl.when(live(unit_g))
        def _():
            pass_on(unit_g, has_next, has_prev, grad_copy, in_g, local_g, out_g)

        @pl.when(jnp.logical_and(live(unit_s), unit_s % PARTS == PARTS - 1))
        def _():
            finish_state(unit_s // PARTS)

        @pl.when(jnp.logical_and(live(unit_g), unit_g % PARTS == PARTS - 1))
        def _():
            finish_grad(unit_g // PARTS)

        return nothing

    lax.fori_loop(0, units + LAG * (sections - 1), step, 0)

    for k in range(chunks):
        rows = slice(k * CHUNK, (k + 1) * CHUNK)
        high, low = split(gscore_ref[k])
        r = r_ref[rows, :]
        w = w_ref[rows, :]
        grads_ref[rows, :state] += dot(
            jnp.concatenate([high, low], axis=0), jnp.concatenate([r, r], axis=0), ((0,), (0,))
        )
        grads_ref[rows, state:] += dot(
            jnp.concatenate([high, low], axis=1), jnp.concatenate([w, w], axis=0), ((1,), (0,))
        )

    share = tokens // group

    def share_copy(gap):
        peer = lax.rem(mine + gap, group)
        return pltpu.make_async_remote_copy(
            src_ref=grads_ref.at[pl.ds(pl.multiple_of(peer * share, share), share)],
            dst_ref=landed_ref.at[gap - 1],
            send_sem=send_h.at[gap - 1],
            recv_sem=recv_h.at[gap - 1],
            device_id={"head": peer},
            device_id_type=MESH,
        )

    for gap in range(1, group):
        share_copy(gap).start()

    def drain(unit, nothing):
        @pl.when(has_next)
        def _():
            state_copy(unit).wait_send()

        @pl.when(has_prev)
        def _():
            grad_copy(unit).wait_send()

        return nothing

    lax.fori_loop(0, units, drain, 0)
    summed = grads_ref[pl.ds(pl.multiple_of(mine * share, share), share)]
    for gap in range(1, group):
        share_copy(gap).wait()
        summed = summed + landed_ref[gap - 1]
    gw_ref[...] = summed[:, :state]
    gr_ref[...] = summed[:, state:]


def per_device(inputs, log_decay, write_proj, read_proj, grad_out):
    tokens, width = inputs.shape
    heads = log_decay.shape[0]
    state = write_proj.shape[1]
    sections = lax.axis_size("seq")
    group = lax.axis_size("head")
    head_size = width // heads
    packs = width // LANES
    chunks = tokens // CHUNK
    units = packs * PARTS
    cumulative = jnp.cumsum(log_decay, axis=1).reshape(packs, LANES // head_size, tokens)
    vmem = pl.BlockSpec(memory_space=pltpu.VMEM)
    block = pltpu.VMEM((packs, state, LANES), F32)
    return pl.pallas_call(
        functools.partial(kernel, sections, group, head_size),
        out_shape=(
            jax.ShapeDtypeStruct((tokens, width), BF16),
            jax.ShapeDtypeStruct((tokens, width), BF16),
            jax.ShapeDtypeStruct((tokens // group, state), F32),
            jax.ShapeDtypeStruct((tokens // group, state), F32),
        ),
        in_specs=[vmem] * 5,
        out_specs=(vmem,) * 4,
        scratch_shapes=[
            pltpu.VMEM((tokens, 2 * state), F32),
            pltpu.VMEM((group - 1, tokens // group, 2 * state), F32),
            pltpu.VMEM((tokens, width), F32),
            pltpu.VMEM((tokens, width), F32),
            pltpu.VMEM((tokens, width), F32),
            pltpu.VMEM((chunks, CHUNK, CHUNK), F32),
            pltpu.VMEM((chunks, CHUNK, CHUNK), F32),
            block, block, block, block, block, block,
            pltpu.SemaphoreType.DMA((units,)),
            pltpu.SemaphoreType.DMA((units,)),
            pltpu.SemaphoreType.DMA((units,)),
            pltpu.SemaphoreType.DMA((units,)),
            pltpu.SemaphoreType.DMA((group - 1,)),
            pltpu.SemaphoreType.DMA((group - 1,)),
        ],
        compiler_params=pltpu.CompilerParams(
            collective_id=0, has_side_effects=True, vmem_limit_bytes=56 * 1024 * 1024
        ),
    )(inputs, grad_out, write_proj, read_proj, cumulative)


def solution(mesh):
    return jax.shard_map(
        per_device,
        mesh=mesh,
        in_specs=(
            P("seq", "head"),
            P("head", "seq"),
            P("seq", None),
            P("seq", None),
            P("seq", "head"),
        ),
        out_specs=(
            P("seq", "head"),
            P("seq", "head"),
            P(("seq", "head"), None),
            P(("seq", "head"), None),
        ),
        check_vma=False,
    )
```

```python
import functools

import jax
import jax.numpy as jnp
from jax import lax
from jax.experimental import pallas as pl
from jax.experimental.pallas import tpu as pltpu
from jax.sharding import PartitionSpec as P

CHUNK = 128
LANES = 128
PARTS = 2
LAG = 3
MESH = pl.DeviceIdType.MESH
F32 = jnp.float32
BF16 = jnp.bfloat16


def dot(a, b, dims):
    return lax.dot_general(a, b, ((dims[0], dims[1]), ((), ())), preferred_element_type=F32)


def split(value):
    high = value.astype(BF16)
    return high, (value - high.astype(F32)).astype(BF16)


def twice(shared, high, low):
    return dot(
        jnp.concatenate([shared, shared], axis=0), jnp.concatenate([high, low], axis=0), ((0,), (0,))
    )


def kernel(
    sections, group, head_size,
    x_ref, g_ref, w_ref, r_ref, cum_ref,
    y_ref, dx_ref, gw_ref, gr_ref,
    grads_ref, landed_ref, decay_ref, y_acc, dx_acc, scores_ref, gscore_ref,
    local_s, local_g, in_s, in_g, out_s, out_g,
    send_s, recv_s, send_g, recv_g, send_h, recv_h,
):
    tokens, width = x_ref.shape
    state = w_ref.shape[1]
    packs = width // LANES
    each = LANES // head_size
    chunks = tokens // CHUNK
    units = packs * PARTS
    part_rows = state // PARTS
    me = lax.axis_index("seq")
    back = sections - 1 - me
    has_prev = me > 0
    has_next = me < sections - 1

    barrier = pltpu.get_barrier_semaphore()

    @pl.when(has_prev)
    def _():
        pl.semaphore_signal(barrier, inc=1, device_id={"seq": me - 1}, device_id_type=MESH)

    @pl.when(has_next)
    def _():
        pl.semaphore_signal(barrier, inc=1, device_id={"seq": me + 1}, device_id_type=MESH)

    mine = lax.axis_index("head")
    for gap in range(1, group):
        pl.semaphore_signal(
            barrier, inc=1, device_id={"head": lax.rem(mine + gap, group)}, device_id_type=MESH
        )
    pl.semaphore_wait(
        barrier, has_prev.astype(jnp.int32) + has_next.astype(jnp.int32) + (group - 1)
    )

    def state_copy(unit):
        pack, rows = unit // PARTS, pl.ds((unit % PARTS) * part_rows, part_rows)
        return pltpu.make_async_remote_copy(
            src_ref=out_s.at[pack, rows],
            dst_ref=in_s.at[pack, rows],
            send_sem=send_s.at[unit],
            recv_sem=recv_s.at[unit],
            device_id={"seq": me + 1},
            device_id_type=MESH,
        )

    def grad_copy(unit):
        pack, rows = unit // PARTS, pl.ds((unit % PARTS) * part_rows, part_rows)
        return pltpu.make_async_remote_copy(
            src_ref=out_g.at[pack, rows],
            dst_ref=in_g.at[pack, rows],
            send_sem=send_g.at[unit],
            recv_sem=recv_g.at[unit],
            device_id={"seq": me - 1},
            device_id_type=MESH,
        )

    @pl.when(me == 0)
    def _():
        in_s[...] = jnp.zeros_like(in_s)

    @pl.when(back == 0)
    def _():
        in_g[...] = jnp.zeros_like(in_g)

    grads_ref[...] = jnp.zeros_like(grads_ref)
    gscore_ref[...] = jnp.zeros_like(gscore_ref)
    for k in range(chunks):
        rows = slice(k * CHUNK, (k + 1) * CHUNK)
        scores_ref[k] = dot(r_ref[rows, :], w_ref[rows, :], ((1,), (1,)))

    lane_head = lax.broadcasted_iota(jnp.int32, (CHUNK, LANES), 1) // head_size
    causal = lax.broadcasted_iota(jnp.int32, (CHUNK, CHUNK), 0) >= lax.broadcasted_iota(
        jnp.int32, (CHUNK, CHUNK), 1
    )

    def only(value, head):
        return jnp.where(lane_head == head, value, jnp.zeros_like(value))

    def local(pack):
        lanes = pl.ds(pl.multiple_of(pack * LANES, LANES), LANES)
        before = jnp.zeros((1, LANES), F32)
        carried = jnp.zeros((state, LANES), F32)
        tails, scaled_x, scaled_g, rest_g, lasts = [], [], [], [], []
        for k in range(chunks):
            rows = slice(k * CHUNK, (k + 1) * CHUNK)
            cum_rows = cum_ref[pack, :, rows]
            spread = jnp.concatenate(
                [jnp.broadcast_to(cum_rows[h : h + 1], (head_size, CHUNK)) for h in range(each)], axis=0
            )
            decay = spread.T
            decay_ref[rows, lanes] = decay
            last = decay[CHUNK - 1 : CHUNK]
            lead = jnp.exp(decay - before)
            tail = jnp.exp(last - decay)
            x = x_ref[rows, lanes]
            g = g_ref[rows, lanes]
            x_tail, x_rest = split(x.astype(F32) * tail)
            g_lead, g_rest = split(g.astype(F32) * lead)
            x_heads = jnp.concatenate([only(x, h) for h in range(each)], axis=0)
            g_heads = jnp.concatenate([only(g, h) for h in range(each)], axis=0)
            product = dot(g, x_heads, ((1,), (1,)))
            mixes, gained = [], gscore_ref[k]
            for h in range(each):
                column = decay[:, h * head_size : h * head_size + 1]
                matrix = jnp.exp(jnp.where(causal, column - cum_rows[h : h + 1], -jnp.inf))
                mixes.append((scores_ref[k] * matrix).astype(BF16))
                gained = gained + product[:, h * CHUNK : (h + 1) * CHUNK] * matrix
            gscore_ref[k] = gained
            y = dot(jnp.concatenate(mixes, axis=1), x_heads, ((1,), (0,)))
            dx = dot(jnp.concatenate(mixes, axis=0), g_heads, ((0,), (0,)))
            dx_acc[rows, lanes] = dx
            if k:
                high, low = split(carried)
                r = r_ref[rows, :]
                y = y + lead * dot(
                    jnp.concatenate([r, r], axis=1), jnp.concatenate([high, low], axis=0), ((1,), (0,))
                )
                grads_ref[rows, state:] += dot(g_lead, high, ((1,), (1,)))
            y_acc[rows, lanes] = y
            carried = jnp.exp(last - before) * carried + twice(w_ref[rows, :], x_tail, x_rest)
            lasts.append(jnp.exp(last - before))
            tails.append(tail)
            scaled_x.append(x_tail)
            scaled_g.append(g_lead)
            rest_g.append(g_rest)
            before = last
        local_s[pack] = carried
        carried = jnp.zeros((state, LANES), F32)
        for k in reversed(range(chunks)):
            rows = slice(k * CHUNK, (k + 1) * CHUNK)
            if k < chunks - 1:
                high, low = split(carried)
                w = w_ref[rows, :]
                dx_acc[rows, lanes] += tails[k] * dot(
                    jnp.concatenate([w, w], axis=1), jnp.concatenate([high, low], axis=0), ((1,), (0,))
                )
                grads_ref[rows, :state] += dot(scaled_x[k], high, ((1,), (1,)))
            carried = lasts[k] * carried + twice(r_ref[rows, :], scaled_g[k], rest_g[k])
        local_g[pack] = carried

    def finish_state(pack):
        lanes = pl.ds(pl.multiple_of(pack * LANES, LANES), LANES)
        high, low = split(in_s[pack])
        both = jnp.concatenate([high, low], axis=0)
        for k in range(chunks):
            rows = slice(k * CHUNK, (k + 1) * CHUNK)
            r = r_ref[rows, :]
            lead = jnp.exp(decay_ref[rows, lanes])
            carried = dot(jnp.concatenate([r, r], axis=1), both, ((1,), (0,)))
            y_ref[rows, lanes] = (y_acc[rows, lanes] + lead * carried).astype(y_ref.dtype)
            g_lead = (g_ref[rows, lanes].astype(F32) * lead).astype(BF16)
            grads_ref[rows, state:] += dot(g_lead, high, ((1,), (1,)))

    def finish_grad(pack):
        lanes = pl.ds(pl.multiple_of(pack * LANES, LANES), LANES)
        high, low = split(in_g[pack])
        both = jnp.concatenate([high, low], axis=0)
        last = decay_ref[tokens - 1 : tokens, lanes]
        for k in range(chunks):
            rows = slice(k * CHUNK, (k + 1) * CHUNK)
            w = w_ref[rows, :]
            tail = jnp.exp(last - decay_ref[rows, lanes])
            carried = dot(jnp.concatenate([w, w], axis=1), both, ((1,), (0,)))
            dx_ref[rows, lanes] = (dx_acc[rows, lanes] + tail * carried).astype(dx_ref.dtype)
            x_tail = (x_ref[rows, lanes].astype(F32) * tail).astype(BF16)
            grads_ref[rows, :state] += dot(x_tail, high, ((1,), (1,)))

    def step(turn, nothing):
        @pl.when(jnp.logical_and(turn % PARTS == 0, turn < units))
        def _():
            local(turn // PARTS)

        unit_s = turn - LAG * me
        unit_g = turn - LAG * back

        def live(unit):
            return jnp.logical_and(unit >= 0, unit < units)

        def pass_on(unit, has_source, has_target, copy, held, local_ref, out_ref):
            pack, rows = unit // PARTS, pl.ds((unit % PARTS) * part_rows, part_rows)
            lanes = pl.ds(pl.multiple_of(pack * LANES, LANES), LANES)

            @pl.when(has_source)
            def _():
                copy(unit).wait_recv()

            @pl.when(has_target)
            def _():
                total = jnp.exp(decay_ref[tokens - 1 : tokens, lanes])
                out_ref[pack, rows] = total * held[pack, rows] + local_ref[pack, rows]
                copy(unit).start()

        @pl.when(live(unit_s))
        def _():
            pass_on(unit_s, has_prev, has_next, state_copy, in_s, local_s, out_s)

        @pl.when(live(unit_g))
        def _():
            pass_on(unit_g, has_next, has_prev, grad_copy, in_g, local_g, out_g)

        @pl.when(jnp.logical_and(live(unit_s), unit_s % PARTS == PARTS - 1))
        def _():
            finish_state(unit_s // PARTS)

        @pl.when(jnp.logical_and(live(unit_g), unit_g % PARTS == PARTS - 1))
        def _():
            finish_grad(unit_g // PARTS)

        @pl.when(turn == units - 1)
        def _():
            for k in range(chunks):
                rows = slice(k * CHUNK, (k + 1) * CHUNK)
                high, low = split(gscore_ref[k])
                r = r_ref[rows, :]
                w = w_ref[rows, :]
                grads_ref[rows, :state] += dot(
                    jnp.concatenate([high, low], axis=0), jnp.concatenate([r, r], axis=0), ((0,), (0,))
                )
                grads_ref[rows, state:] += dot(
                    jnp.concatenate([high, low], axis=1), jnp.concatenate([w, w], axis=0), ((1,), (0,))
                )

        return nothing

    lax.fori_loop(0, units + LAG * (sections - 1), step, 0)

    share = tokens // group

    def share_copy(gap):
        peer = lax.rem(mine + gap, group)
        return pltpu.make_async_remote_copy(
            src_ref=grads_ref.at[pl.ds(pl.multiple_of(peer * share, share), share)],
            dst_ref=landed_ref.at[gap - 1],
            send_sem=send_h.at[gap - 1],
            recv_sem=recv_h.at[gap - 1],
            device_id={"head": peer},
            device_id_type=MESH,
        )

    for gap in range(1, group):
        share_copy(gap).start()

    def drain(unit, nothing):
        @pl.when(has_next)
        def _():
            state_copy(unit).wait_send()

        @pl.when(has_prev)
        def _():
            grad_copy(unit).wait_send()

        return nothing

    lax.fori_loop(0, units, drain, 0)
    summed = grads_ref[pl.ds(pl.multiple_of(mine * share, share), share)]
    for gap in range(1, group):
        share_copy(gap).wait()
        summed = summed + landed_ref[gap - 1]
    gw_ref[...] = summed[:, :state]
    gr_ref[...] = summed[:, state:]


def per_device(inputs, log_decay, write_proj, read_proj, grad_out):
    tokens, width = inputs.shape
    heads = log_decay.shape[0]
    state = write_proj.shape[1]
    sections = lax.axis_size("seq")
    group = lax.axis_size("head")
    head_size = width // heads
    packs = width // LANES
    chunks = tokens // CHUNK
    units = packs * PARTS
    cumulative = jnp.cumsum(log_decay, axis=1).reshape(packs, LANES // head_size, tokens)
    vmem = pl.BlockSpec(memory_space=pltpu.VMEM)
    block = pltpu.VMEM((packs, state, LANES), F32)
    return pl.pallas_call(
        functools.partial(kernel, sections, group, head_size),
        out_shape=(
            jax.ShapeDtypeStruct((tokens, width), BF16),
            jax.ShapeDtypeStruct((tokens, width), BF16),
            jax.ShapeDtypeStruct((tokens // group, state), F32),
            jax.ShapeDtypeStruct((tokens // group, state), F32),
        ),
        in_specs=[vmem] * 5,
        out_specs=(vmem,) * 4,
        scratch_shapes=[
            pltpu.VMEM((tokens, 2 * state), F32),
            pltpu.VMEM((group - 1, tokens // group, 2 * state), F32),
            pltpu.VMEM((tokens, width), F32),
            pltpu.VMEM((tokens, width), F32),
            pltpu.VMEM((tokens, width), F32),
            pltpu.VMEM((chunks, CHUNK, CHUNK), F32),
            pltpu.VMEM((chunks, CHUNK, CHUNK), F32),
            block, block, block, block, block, block,
            pltpu.SemaphoreType.DMA((units,)),
            pltpu.SemaphoreType.DMA((units,)),
            pltpu.SemaphoreType.DMA((units,)),
            pltpu.SemaphoreType.DMA((units,)),
            pltpu.SemaphoreType.DMA((group - 1,)),
            pltpu.SemaphoreType.DMA((group - 1,)),
        ],
        compiler_params=pltpu.CompilerParams(
            collective_id=0, has_side_effects=True, vmem_limit_bytes=56 * 1024 * 1024
        ),
    )(inputs, grad_out, write_proj, read_proj, cumulative)


def solution(mesh):
    return jax.shard_map(
        per_device,
        mesh=mesh,
        in_specs=(
            P("seq", "head"),
            P("head", "seq"),
            P("seq", None),
            P("seq", None),
            P("seq", "head"),
        ),
        out_specs=(
            P("seq", "head"),
            P("seq", "head"),
            P(("seq", "head"), None),
            P(("seq", "head"), None),
        ),
        check_vma=False,
    )
```
